256 devices in a mesh: row: 8 (over y, z_hi), col: 8 (over x, core), pack: 4 (over z_lo).
Axes of the slice: x: 4, y: 4, z: 8 (z_hi: 2, z_lo: 4; z = z_hi * 4 + z_lo), core: 2. Of those that a mesh axis runs over, the one named last changes fastest.
Arguments:
- giant_emb: bfloat16 [32768, 1024], P(('row', 'col', 'pack')), may hold values from -8 to 8
- small_emb: bfloat16 [262144, 1024], P(('row', 'col', 'pack')), may hold values from -8 to 8
- small_ids: int32 [262144], P(('row', 'col', 'pack')), may hold values from 0 to 128, as said below
- send_rows: int32 [32768], P(('row', 'col', 'pack')), may hold values from 0 to 1023
- target_rows: int32 [32768], P(('row', 'col', 'pack')), may hold values from 0 to 1023, as said below
Outputs:
- giant_max: float32 [32768], P(('row', 'col', 'pack'))
- small_max: float32 [262144], P(('row', 'col', 'pack'))
The draws below stay inside these ranges and needn't reach their ends.
Inputs may be any that keep to these rules, and one draw needn't show every extreme that they name: `small_ids`: within each block of 1024 rows the ids are nondecreasing, so members of one cluster are contiguous. `target_rows`: the 128 entries of one block are distinct.
All inputs are finite; a program needn't handle non-finite values.
Results may differ from the reference program's by a relative error of at most 0.002.
Values may be sent and summed in bfloat16 or wider, within the bound.
No kernel may reach another device: no remote copies, remote signals or barrier semaphores. Data moves between devices by JAX's collectives and lax.ppermute only.
A program may use at most 64 MiB of HBM per device.

```python
import math
import jax
import jax.numpy as jnp
from jax import lax

D = 1024
SMALL_DEV = 1024
BOUND_DEV = 128
GK = 32768
SN = 262144
RUN = 4
DEVICES = 256


def pair_rows(key):
    key_send, key_target = jax.random.split(key)
    send_rows = jax.random.randint(key_send, (DEVICES * BOUND_DEV,), 0, SMALL_DEV)
    block_keys = jax.random.split(key_target, DEVICES)
    target_rows = jax.vmap(lambda one_key: jax.random.permutation(one_key, SMALL_DEV)[:BOUND_DEV])(block_keys)
    return (send_rows, target_rows.reshape(DEVICES * BOUND_DEV).astype(jnp.int32))


def base_rows(key, shape):
    key_base = jax.random.fold_in(key, 0)
    return jax.random.normal(key_base, shape, jnp.float32)


def draw_giant_emb(key, part):
    key = jax.random.fold_in(key, 5)
    key_base, key_source, key_flag, key_weight, key_noise = jax.random.split(key, 5)
    base = base_rows(key_base, (GK, D))
    positions = jnp.arange(GK, dtype=jnp.int32)
    source = jax.random.randint(key_source, (GK,), 0, jnp.maximum(positions, 1))
    flag = jax.random.randint(key_flag, (GK,), 0, 2).astype(jnp.float32)[:, None]
    weight = jax.random.uniform(key_weight, (GK, 1), jnp.float32, 0.5, 3.0)
    noise = jax.random.normal(key_noise, (GK, D), jnp.float32)
    copied = weight * jnp.take(base, source, axis=0) + noise
    return jnp.clip(flag * copied + (1.0 - flag) * base, -8.0, 8.0).astype(jnp.bfloat16)


def draw_small_emb(key, part):
    send_rows, target_rows = pair_rows(key)
    key = jax.random.fold_in(key, 11)
    key_base, key_back, key_flag, key_weight, key_noise, key_bweight, key_bnoise = jax.random.split(key, 7)
    base = base_rows(key_base, (DEVICES, SMALL_DEV, D))
    positions = jnp.arange(SMALL_DEV, dtype=jnp.int32)
    back_steps = jax.random.randint(key_back, (DEVICES, SMALL_DEV), 1, 4)
    source = jnp.maximum(positions[None, :] - back_steps, 0)
    flag = jax.random.randint(key_flag, (DEVICES, SMALL_DEV), 0, 2).astype(jnp.float32)[:, :, None]
    weight = jax.random.uniform(key_weight, (DEVICES, SMALL_DEV, 1), jnp.float32, 0.5, 3.0)
    noise = jax.random.normal(key_noise, (DEVICES, SMALL_DEV, D), jnp.float32)
    copied = weight * jnp.take_along_axis(base, source[:, :, None], axis=1) + noise
    values = flag * copied + (1.0 - flag) * base
    blocks = jnp.arange(DEVICES, dtype=jnp.int32)
    place = blocks % RUN
    sender = blocks - place + (place + RUN - 1) % RUN
    send_blocks = send_rows.reshape(DEVICES, BOUND_DEV)
    target_blocks = target_rows.reshape(DEVICES, BOUND_DEV)
    sources = base[sender[:, None], send_blocks[sender]]
    bound_weight = jax.random.uniform(key_bweight, (DEVICES, BOUND_DEV, 1), jnp.float32, 0.5, 3.0)
    bound_noise = jax.random.normal(key_bnoise, (DEVICES, BOUND_DEV, D), jnp.float32)
    values = values.at[blocks[:, None], target_blocks].set(bound_weight * sources + bound_noise)
    return jnp.clip(values, -8.0, 8.0).reshape(SN, D).astype(jnp.bfloat16)


def draw_small_ids(key, part):
    key = jax.random.fold_in(key, 17)
    starts = (jax.random.randint(key, (DEVICES, SMALL_DEV), 0, 8) == 0).astype(jnp.int32)
    positions = jnp.arange(SMALL_DEV, dtype=jnp.int32)
    forced = (jnp.arange(DEVICES, dtype=jnp.int32)[:, None] == 0) & (positions[None, :] < SMALL_DEV // 8)
    starts = jnp.where(forced, 1, starts)
    ids = jnp.minimum(jnp.cumsum(starts, axis=1), SMALL_DEV // 8)
    return ids.astype(jnp.int32).reshape(SN)


def draw_send_rows(key, part):
    return pair_rows(key)[0]


def draw_target_rows(key, part):
    return pair_rows(key)[1]


def setup_inputs(seed: int = 0) -> dict:
    keys = jax.random.split(jax.random.key(seed), 6)
    giant_emb = draw_giant_emb(jax.random.fold_in(keys[5], 71), 0)
    small_emb = draw_small_emb(jax.random.fold_in(keys[5], 71), 0)
    small_ids = draw_small_ids(jax.random.fold_in(keys[5], 71), 0)
    send_rows = draw_send_rows(jax.random.fold_in(keys[5], 71), 0)
    target_rows = draw_target_rows(jax.random.fold_in(keys[5], 71), 0)
    return {"giant_emb": giant_emb, "small_emb": small_emb, "small_ids": small_ids, "send_rows": send_rows, "target_rows": target_rows}


def to_unit(values):
    wide = values.astype(jnp.float32)
    inverse = lax.rsqrt(lax.optimization_barrier(jnp.sum(wide * wide, axis=-1, keepdims=True)) + 1e-06)
    return (wide * inverse).astype(jnp.bfloat16)

def reference(giant_emb, small_emb, small_ids, send_rows, target_rows):
    giant_unit = to_unit(giant_emb)
    block_size = math.gcd(GK, 256)
    all_positions = jnp.arange(GK, dtype=jnp.int32)

    def giant_block(first_row):
        block_rows = lax.dynamic_slice_in_dim(giant_unit, first_row, block_size, 0)
        scores = jnp.dot(block_rows, giant_unit.T, preferred_element_type=jnp.float32)
        row_positions = first_row + jnp.arange(block_size, dtype=jnp.int32)
        allowed = all_positions[None, :] < row_positions[:, None]
        return lax.optimization_barrier(jnp.max(jnp.where(allowed, scores, jnp.float32(-1.0)), axis=1))
    starts = jnp.arange(GK // block_size, dtype=jnp.int32) * block_size
    giant_max = lax.map(giant_block, starts).reshape(GK)
    small_unit = to_unit(small_emb).reshape(DEVICES, SMALL_DEV, D)
    ids_blocks = small_ids.reshape(DEVICES, SMALL_DEV)
    send_blocks = send_rows.reshape(DEVICES, BOUND_DEV)
    target_blocks = target_rows.reshape(DEVICES, BOUND_DEV)
    blocks = jnp.arange(DEVICES, dtype=jnp.int32)
    place = blocks % RUN
    sender = blocks - place + (place + RUN - 1) % RUN
    receiver = blocks - place + (place + 1) % RUN
    outgoing = jnp.take_along_axis(small_unit, send_blocks[:, :, None], axis=1)
    incoming = outgoing[sender]
    member_pos = jnp.arange(SMALL_DEV, dtype=jnp.int32)

    def small_block(inputs):
        members, ids_here, arriving, targets = inputs
        scores = jnp.dot(members, members.T, preferred_element_type=jnp.float32)
        allowed = (ids_here[:, None] == ids_here[None, :]) & (member_pos[None, :] < member_pos[:, None])
        local_max = lax.optimization_barrier(jnp.max(jnp.where(allowed, scores, jnp.float32(-1.0)), axis=1))
        cross = jnp.dot(arriving, members.T, preferred_element_type=jnp.float32)
        target_ids = jnp.take(ids_here, targets)
        cross = jnp.where(target_ids[:, None] == ids_here[None, :], cross, jnp.float32(-1.0))
        return (local_max, lax.optimization_barrier(jnp.max(cross, axis=0)), lax.optimization_barrier(jnp.max(cross, axis=1)))
    local_max, toward_max, back_max = lax.map(small_block, (small_unit, ids_blocks, incoming, target_blocks))
    returned = back_max[receiver]
    hits = send_blocks[:, :, None] == member_pos[None, None, :]
    returned_max = lax.optimization_barrier(jnp.max(jnp.where(hits, returned[:, :, None], jnp.float32(-1.0)), axis=1))
    small_max = jnp.maximum(jnp.maximum(local_max, toward_max), returned_max).reshape(SN)
    return (giant_max, small_max)
```

```python
import functools
import jax
import jax.numpy as jnp
from jax import lax
from jax.experimental import pallas as pl
from jax.experimental.pallas import tpu as pltpu
from jax.sharding import PartitionSpec as P

AXES = ("row", "col", "pack")
LOW = -2.0
NT = (((1,), (1,)), ((), ()))


def place(x, y, z, c):
    return ((y * 2 + z // 4) * 8 + x * 2 + c) * 4 + z % 4


def z_even(x, y, z):
    return x, y, z ^ 1


def z_odd(x, y, z):
    return x, y, ((z + 7) % 8 if z % 2 == 0 else (z + 1) % 8)


MOVES = {
    "x0": lambda x, y, z: (x ^ 1, y, z),
    "x1": lambda x, y, z: (x ^ 3, y, z),
    "y0": lambda x, y, z: (x, y ^ 1, z),
    "y1": lambda x, y, z: (x, y ^ 3, z),
    "z0": z_even,
    "z1": z_odd,
}
ORDER = {
    "a": (("x0", "y0", "x1", "y1"), ("y0", "x0", "y1", "x1")),
    "b": (("x1", "y1", "x0", "y0"), ("y1", "x1", "y0", "x0")),
    "z": (("z0", "z1", "z0", "z1"), ("z1", "z0", "z1", "z0")),
}


def exchange(block, stream, step):
    route = []
    for x in range(4):
        for y in range(4):
            for z in range(8):
                for c in range(2):
                    to = MOVES[ORDER[stream][c][step]](x, y, z)
                    route.append((place(x, y, z, c), place(*to, c)))
    return lax.ppermute(block, AXES, route)


def core_swap(block):
    route = [
        (place(x, y, z, c), place(x, y, z, 1 - c))
        for x in range(4) for y in range(4) for z in range(8) for c in range(2)
    ]
    return lax.ppermute(block, AXES, route)


def unit_kernel(values_ref, out_ref):
    wide = values_ref[...].astype(jnp.float32)
    inverse = lax.rsqrt(jnp.sum(wide * wide, axis=-1, keepdims=True) + 1e-06)
    out_ref[...] = (wide * inverse).astype(jnp.bfloat16)


def unit_call(values):
    return pl.pallas_call(
        unit_kernel,
        out_shape=jax.ShapeDtypeStruct(values.shape, jnp.bfloat16),
        in_specs=[pl.BlockSpec(memory_space=pltpu.VMEM)],
        out_specs=pl.BlockSpec(memory_space=pltpu.VMEM),
        compiler_params=pltpu.CompilerParams(vmem_limit_bytes=32 * 1024 * 1024),
    )(values)


def tile_kernel(n_r, n_c, r_starts, c_starts, *refs):
    r_refs, c_refs, out_ref = refs[:n_r], refs[n_r : n_r + n_c], refs[-1]
    lane = lax.broadcasted_iota(jnp.int32, (1, 256), 1)
    sub = lax.broadcasted_iota(jnp.int32, (128, 256), 0)
    base = 0
    for r_ref in r_refs:
        for j in range(r_ref.shape[0] // 256):
            rows = r_ref[256 * j : 256 * (j + 1), :]
            first = (base + 256 * j) // 64
            row_pos = r_starts[first] + lane
            for k in range(1, 4):
                row_pos = jnp.where(lane >= 64 * k, r_starts[first + k] + lane - 64 * k, row_pos)
            best = jnp.full((8, 256), LOW, jnp.float32)
            for i, c_ref in enumerate(c_refs):
                scores = lax.dot_general(c_ref[...], rows, NT, preferred_element_type=jnp.float32)
                for h in range(2):
                    limit = row_pos - c_starts[2 * i + h]
                    part = jnp.where(sub < limit, scores[128 * h : 128 * (h + 1)], LOW)
                    best = jnp.maximum(best, jnp.max(part.reshape(16, 8, 256), axis=0))
            out_ref[:, base + 256 * j : base + 256 * (j + 1)] = jnp.max(best, axis=0, keepdims=True)
        base += r_ref.shape[0]


def tile_max(r_list, r_starts, c_list, c_starts):
    rows = sum(r.shape[0] for r in r_list)
    cols = sum(c.shape[0] for c in c_list)
    smem = pl.BlockSpec(memory_space=pltpu.SMEM)
    vmem = pl.BlockSpec(memory_space=pltpu.VMEM)
    return pl.pallas_call(
        functools.partial(tile_kernel, len(r_list), len(c_list)),
        out_shape=jax.ShapeDtypeStruct((1, rows), jnp.float32),
        in_specs=[smem, smem] + [vmem] * (len(r_list) + len(c_list)),
        out_specs=vmem,
        compiler_params=pltpu.CompilerParams(vmem_limit_bytes=40 * 1024 * 1024),
        cost_estimate=pl.CostEstimate(
            flops=2 * rows * cols * 1024, bytes_accessed=(rows + cols) * 2048, transcendentals=0
        ),
    )(r_starts, c_starts, *r_list, *c_list)


def giant_part(giant_emb):
    rows = giant_emb.shape[0]
    half = rows // 2
    row_index, col_index, z_low = (lax.axis_index(a) for a in AXES)
    x, core = col_index // 2, col_index % 2
    y, z = row_index // 2, (row_index % 2) * 4 + z_low
    unit = unit_call(giant_emb)

    spot = jnp.arange(16, dtype=jnp.int32)
    bit = [(spot >> k) & 1 for k in range(4)]

    def plane_starts(x_bits, y_bits):
        xs = x ^ bit[x_bits[0]] ^ (3 * bit[x_bits[1]])
        ys = y ^ bit[y_bits[0]] ^ (3 * bit[y_bits[1]])
        return place(xs, ys, z, core) * rows

    first = core == 0
    a_starts = jnp.where(first, plane_starts((0, 2), (1, 3)), plane_starts((1, 3), (0, 2)))
    b_starts = jnp.where(first, plane_starts((2, 0), (3, 1)), plane_starts((3, 1), (2, 0))) + half

    def line_starts(zz, cc):
        def step(v, odd):
            up = (v % 2 == 0) != odd
            return jnp.where(up, (v + 1) % 8, (v + 7) % 8)
        o0 = cc == 1
        o1 = cc == 0
        z1 = step(zz, o0)
        q = step(zz, o1)
        r = step(z1, o1)
        s = step(step(q, o0), o1)
        order = [zz, z1, q, step(q, o0), r, step(r, o0), s, step(s, o0)]
        return jnp.stack([place(x, y, v, cc) * rows for v in order])

    own_starts, other_starts = line_starts(z, core), line_starts(z, 1 - core)

    a, b = unit[:half], unit[half:]
    a1, b1, c1 = exchange(a, "a", 0), exchange(b, "b", 0), exchange(unit, "z", 0)
    a, b, c01 = jnp.concatenate([a, a1]), jnp.concatenate([b, b1]), jnp.concatenate([unit, c1])
    a2, b2, c2 = exchange(a, "a", 1), exchange(b, "b", 1), exchange(c01, "z", 1)
    s01 = core_swap(c01)
    a, b = jnp.concatenate([a, a2]), jnp.concatenate([b, b2])
    a3, b3, c3 = exchange(a, "a", 2), exchange(b, "b", 2), exchange(c2, "z", 2)
    s2 = core_swap(c2)
    a, b = jnp.concatenate([a, a3]), jnp.concatenate([b, b3])
    a4, b4, c4 = exchange(a, "a", 3), exchange(b, "b", 3), exchange(c3, "z", 3)
    s3 = core_swap(c3)
    near_starts = jnp.concatenate([a_starts[:8], b_starts[:8]])
    starts1 = jnp.concatenate([own_starts[:4], other_starts[:4]])
    starts2 = jnp.concatenate([own_starts[4:], other_starts[4:]])
    near = tile_max([a, b], near_starts, [c01, c2, s01, s2], starts1)
    s4 = core_swap(c4)
    near = jnp.maximum(near, tile_max([a, b], near_starts, [c3, c4, s3, s4], starts2))
    every, every_starts = [c01, c2, s01, s2, c3, c4, s3, s4], jnp.concatenate([starts1, starts2])
    far_a = tile_max([a4], a_starts[8:], every, every_starts)
    far_b = tile_max([b4], b_starts[8:], every, every_starts)
    near = near.reshape(2, 8, half)
    best_a = jnp.concatenate([near[0], far_a.reshape(8, half)])
    best_b = jnp.concatenate([near[1], far_b.reshape(8, half)])
    best_b = best_b.reshape(2, 2, 2, 2, half).transpose(2, 3, 0, 1, 4).reshape(16, half)
    best = jnp.concatenate([best_a, best_b], axis=1)
    for step in (3, 2, 1, 0):
        kept = best.shape[0] // 2
        best = jnp.maximum(best[:kept], exchange(best[kept:], "a", step))
    return jnp.maximum(best.reshape(rows), jnp.float32(-1.0))


def to_unit(values):
    wide = values.astype(jnp.float32)
    inverse = lax.rsqrt(jnp.sum(wide * wide, axis=-1, keepdims=True) + 1e-06)
    return (wide * inverse).astype(jnp.bfloat16)


def shifted(block, axis, distance):
    devices = range(lax.axis_size(axis))
    route = [((i - distance) % len(devices), i) for i in devices]
    return lax.ppermute(block, axis, route)


def small_part(small_emb, small_ids, send_rows, target_rows):
    small_unit = to_unit(small_emb)
    block_size = small_unit.shape[0]
    outgoing = jnp.take(small_unit, send_rows, axis=0, mode="clip")
    incoming = shifted(outgoing, "pack", 1)
    member_pos = jnp.arange(block_size, dtype=jnp.int32)
    local_scores = jnp.einsum("id,jd->ij", small_unit, small_unit, preferred_element_type=jnp.float32)
    local_allowed = (small_ids[:, None] == small_ids[None, :]) & (member_pos[None, :] < member_pos[:, None])
    local_max = jnp.max(jnp.where(local_allowed, local_scores, jnp.float32(-1.0)), axis=1)
    cross = jnp.einsum("td,id->ti", incoming, small_unit, preferred_element_type=jnp.float32)
    target_ids = jnp.take(small_ids, target_rows, mode="clip")
    cross = jnp.where(target_ids[:, None] == small_ids[None, :], cross, jnp.float32(-1.0))
    toward_max = jnp.max(cross, axis=0)
    back_max = jnp.max(cross, axis=1)
    returned = shifted(back_max, "pack", -1)
    hits = send_rows[:, None] == member_pos[None, :]
    returned_max = jnp.max(jnp.where(hits, returned[:, None], jnp.float32(-1.0)), axis=0)
    return jnp.maximum(jnp.maximum(local_max, toward_max), returned_max)


def body(giant_emb, small_emb, small_ids, send_rows, target_rows):
    return giant_part(giant_emb), small_part(small_emb, small_ids, send_rows, target_rows)


def solution(mesh):
    spread = P(AXES)
    wide = P(AXES, None)
    return jax.shard_map(
        body,
        mesh=mesh,
        in_specs=(wide, wide, spread, spread, spread),
        out_specs=(spread, spread),
        check_vma=False,
    )
```

```python
import functools
import jax
import jax.numpy as jnp
from jax import lax
from jax.experimental import pallas as pl
from jax.experimental.pallas import tpu as pltpu
from jax.sharding import PartitionSpec as P

AXES = ("row", "col", "pack")
LOW = -2.0
NT = (((1,), (1,)), ((), ()))
MIB = 1024 * 1024
SMEM = pl.BlockSpec(memory_space=pltpu.SMEM)
VMEM = pl.BlockSpec(memory_space=pltpu.VMEM)
LATER = pl.BlockSpec(memory_space=pl.ANY)


def place(x, y, z, c):
    return ((y * 2 + z // 4) * 8 + x * 2 + c) * 4 + z % 4


def z_step(z, odd):
    return (z + 1 + 6 * ((z + odd) % 2)) % 8


def partner(link, x, y, z, c):
    if link in ("E", "O"):
        return x, y, z_step(z, (link == "O") != (c == 1))
    flip = 1 if link[0] == "P" else 3
    along_x = (len(link) == 1) == (c == 0)
    return (x ^ flip, y, z) if along_x else (x, y ^ flip, z)


def route(move):
    cells = [(x, y, z, c) for x in range(4) for y in range(4) for z in range(8) for c in range(2)]
    return [(place(*cell), place(*move(*cell))) for cell in cells]


def over(block, link):
    return lax.ppermute(block, AXES, route(lambda x, y, z, c: (*partner(link, x, y, z, c), c)))


def core_swap(block):
    return lax.ppermute(block, AXES, route(lambda x, y, z, c: (x, y, z, 1 - c)))


def call(kernel, out_shape, specs, operands, after=(), flops=0, size=0):
    n = len(operands)

    def run(*refs):
        kernel(*refs[:n], *refs[n + len(after) :])

    many = isinstance(out_shape, (tuple, list))
    return pl.pallas_call(
        run,
        out_shape=out_shape,
        in_specs=list(specs) + [LATER] * len(after),
        out_specs=[VMEM] * len(out_shape) if many else VMEM,
        compiler_params=pltpu.CompilerParams(vmem_limit_bytes=8 * MIB),
        cost_estimate=pl.CostEstimate(flops=flops, bytes_accessed=size, transcendentals=0),
    )(*operands, *after)


def shape(rows, columns, dtype):
    return jax.ShapeDtypeStruct((rows, columns), dtype)


def dot_nt(left, right):
    total = None
    for k in range(0, 1024, 256):
        part = lax.dot_general(left[:, k : k + 256], right[:, k : k + 256], NT, preferred_element_type=jnp.float32)
        total = part if total is None else total + part
    return total


def unit_rows(values):
    wide = values.astype(jnp.float32)
    inverse = lax.rsqrt(jnp.sum(wide * wide, axis=-1, keepdims=True) + 1e-06)
    return (wide * inverse).astype(jnp.bfloat16)


def unit_kernel(values, out):
    for i in range(0, values.shape[0], 128):
        out[i : i + 128, :] = unit_rows(values[i : i + 128, :])


def join_kernel(first, second, out):
    rows = first.shape[0]
    out[:rows, :] = first[...]
    out[rows:, :] = second[...]


def join(first, second, after=()):
    rows = first.shape[0] + second.shape[0]
    return call(join_kernel, shape(rows, 1024, jnp.bfloat16), [VMEM] * 2, [first, second], after, size=rows * 4096)


def here():
    row_index, col_index, z_low = (lax.axis_index(a) for a in AXES)
    return col_index >> 1, row_index >> 1, ((row_index & 1) << 2) | z_low, col_index & 1


def first_row(x, y, z, c):
    return ((((((y << 1) | (z >> 2)) << 3) | (x << 1) | c) << 2) | (z & 3)) << 7


def plane_start(at, far, near):
    x, y, z, core = at
    flip = (0, 1, 3, 2)
    if far == near:
        along_x = along_y = flip[far]
    else:
        along_x = jnp.where(core == 0, flip[near], flip[far])
        along_y = jnp.where(core == 0, flip[far], flip[near])
    return first_row(x ^ along_x, y ^ along_y, z, core)


def line_start(at, steps, other):
    x, y, z, core = at
    core = (1 - core) if other else core
    way = 1 - 2 * ((z + core) & 1)
    return first_row(x, y, (z + way * steps + 8) & 7, core)


def tile_kernel(row_names, col_names, n_before, spots, *refs):
    at = here()
    n_r, n_c = len(row_names), len(col_names)
    r_refs, c_refs = refs[:n_r], refs[n_r : n_r + n_c]
    before, outs = refs[n_r + n_c : n_r + n_c + n_before], refs[n_r + n_c + n_before :]
    out_rows = outs[0].shape[0]
    lane = lax.broadcasted_iota(jnp.int32, (1, 256), 1)
    sub = lax.broadcasted_iota(jnp.int32, (128, 256), 0)
    starts = [[line_start(at, name + h if name >= 0 else name - h, other) for h in range(2)] for name, other in col_names]
    for j, (r_ref, (far, near)) in enumerate(zip(r_refs, row_names)):
        row_pos = jnp.where(lane < 128, plane_start(at, far, near) + lane, plane_start(at, far, near + 1) + lane - 128)
        best = jnp.full((8, 256), LOW, jnp.float32)
        for i in range(n_c):
            scores = dot_nt(c_refs[i], r_ref)
            for h in range(2):
                kept = jnp.where(sub < row_pos - starts[i][h], scores[128 * h : 128 * (h + 1)], LOW)
                best = jnp.maximum(best, jnp.max(kept.reshape(16, 8, 256), axis=0))
        best = jnp.max(best, axis=0, keepdims=True)
        for h in range(2):
            spot = 2 * j + h
            value = best[:, 128 * h : 128 * (h + 1)]
            seen = 0
            for b in before:
                if seen <= spot < seen + b.shape[0]:
                    value = jnp.maximum(value, b[spot - seen : spot - seen + 1, :])
                seen += b.shape[0]
            spot = 2 * spots[j] + h
            outs[spot // out_rows][spot % out_rows : spot % out_rows + 1, :] = value


def tile(rows, cols, before=(), after=(), spots=None):
    n = 2 * len(rows)
    out = shape(n, 128, jnp.float32) if spots is None else [shape(n // 2, 128, jnp.float32)] * 2
    operands = [*rows.values(), *cols.values(), *before]
    return call(
        functools.partial(tile_kernel, list(rows), list(cols), len(before), spots or range(len(rows))),
        out, [VMEM] * len(operands), operands, after,
        flops=2 * n * 128 * len(cols) * 256 * 1024, size=(n + 2 * len(cols)) * 256 * 1024,
    )


def fold_kernel(mine, theirs, *outs):
    best = jnp.maximum(mine[...], theirs[...])
    if len(outs) == 1:
        outs[0][...] = jnp.maximum(best, -1.0)
    else:
        half = best.shape[0] // 2
        outs[0][...] = best[:half]
        outs[1][...] = best[half:]


def fold(mine, theirs):
    half = mine.shape[0] // 2
    out = [shape(half, 128, jnp.float32)] * 2 if half else shape(1, 128, jnp.float32)
    return call(fold_kernel, out, [VMEM] * 2, [mine, theirs])


def column(row):
    return jnp.broadcast_to(row, (128, 128)).T


def gather_kernel(unit, send, out):
    lane = lax.broadcasted_iota(jnp.int32, (128, 128), 1)
    wanted = column(send[...])
    total = None
    for k in range(0, 1024, 256):
        hit = jnp.concatenate([wanted == lane + k, wanted == lane + k + 128], axis=1)
        part = jnp.dot(hit.astype(jnp.bfloat16), unit[k : k + 256, :], preferred_element_type=jnp.float32)
        total = part if total is None else total + part
    out[...] = total.astype(jnp.bfloat16)


def local_kernel(unit, ids, out):
    sub = lax.broadcasted_iota(jnp.int32, (256, 256), 0)
    lane = lax.broadcasted_iota(jnp.int32, (256, 256), 1)
    id_col = []
    for j in range(4):
        parts = [column(ids[:, 256 * j + 128 * h : 256 * j + 128 * (h + 1)]) for h in range(2)]
        part = jnp.concatenate(parts)
        id_col.append(jnp.concatenate([part, part], axis=1))
    for i in range(4):
        rows = slice(256 * i, 256 * (i + 1))
        best = jnp.full((8, 256), -1.0, jnp.float32)
        for j in range(i + 1):
            scores = dot_nt(unit[256 * j : 256 * (j + 1), :], unit[rows, :])
            allowed = id_col[j] == ids[:, rows]
            if i == j:
                allowed = allowed & (sub < lane)
            scores = jnp.where(allowed, scores, -1.0)
            best = jnp.maximum(best, jnp.max(scores.reshape(32, 8, 256), axis=0))
        out[:, rows] = jnp.max(best, axis=0, keepdims=True)


def cross_kernel(incoming, unit, ids, target, toward, back):
    lane = lax.broadcasted_iota(jnp.int32, (128, 128), 1)
    wanted = column(target[...])
    found = jnp.zeros((128, 128), jnp.int32)
    for k in range(0, 1024, 128):
        found = found + jnp.where(wanted == lane + k, ids[:, k : k + 128], 0)
    target_id = jnp.sum(found, axis=1, keepdims=True)
    back_best = jnp.full((128, 128), -1.0, jnp.float32)
    for i in range(0, 1024, 256):
        scores = dot_nt(incoming[...], unit[i : i + 256, :])
        scores = jnp.where(target_id == ids[:, i : i + 256], scores, -1.0)
        toward[:, i : i + 256] = jnp.max(scores, axis=0, keepdims=True)
        back_best = jnp.maximum(back_best, jnp.maximum(scores[:, :128], scores[:, 128:]))
    back[...] = jnp.max(back_best.T, axis=0, keepdims=True)


def finish_kernel(returned, send, local, toward, out):
    lane = lax.broadcasted_iota(jnp.int32, (128, 128), 1)
    wanted, value = column(send[...]), column(returned[...])
    for k in range(0, 1024, 128):
        hit = jnp.max(jnp.where(wanted == lane + k, value, -1.0), axis=0, keepdims=True)
        out[:, k : k + 128] = jnp.maximum(jnp.maximum(local[:, k : k + 128], toward[:, k : k + 128]), hit)


def pack_shift(block, distance):
    size = lax.axis_size("pack")
    return lax.ppermute(block, "pack", [((i - distance) % size, i) for i in range(size)])


def body(giant_emb, small_emb, small_ids, send_rows, target_rows):
    ids, send, target = small_ids.reshape(1, 1024), send_rows.reshape(1, 128), target_rows.reshape(1, 128)

    own = call(unit_kernel, shape(128, 1024, jnp.bfloat16), [VMEM], [giant_emb])
    e, p, q = over(own, "E"), over(own, "P"), over(own, "Q")
    small = call(unit_kernel, shape(1024, 1024, jnp.bfloat16), [VMEM], [small_emb], [own], size=4 * MIB)
    c1 = join(own, e, [small])
    c2, d1 = over(c1, "O"), core_swap(c1)
    a = join(own, p, [c1])
    pq = over(p, "Q")
    a_p, a_q = over(a, "P2"), over(a, "Q2")
    local = call(local_kernel, shape(1, 1024, jnp.float32), [VMEM] * 2, [small, ids], [a], flops=20 * 2**26)
    b = join(q, pq, [local])
    b_p, b_q = over(b, "P2"), over(b, "Q2")
    outgoing = call(gather_kernel, shape(128, 1024, jnp.bfloat16), [VMEM] * 2, [small, send], [b], flops=2**28)
    one = tile({(0, 0): a, (0, 2): b}, {(0, False): c1, (0, True): d1}, after=[outgoing])
    a_pq = over(a_p, "Q2")
    c3, d2 = over(c2, "E"), core_swap(c2)
    two = tile(
        {(1, 0): a_p, (2, 0): a_q}, {(0, False): c1, (0, True): d1, (-1, False): c2, (-1, True): d2}, after=[one],
    )
    b_pq = over(b_q, "P2")
    three = tile(
        {(1, 2): b_p, (2, 2): b_q}, {(0, False): c1, (0, True): d1, (-1, False): c2, (-1, True): d2}, after=[two],
    )
    one = tile({(0, 0): a, (0, 2): b}, {(-1, False): c2, (-1, True): d2}, [one], after=[three])
    c4, d3 = over(c3, "O"), core_swap(c3)
    incoming = pack_shift(outgoing, 1)
    four = tile(
        {(3, 0): a_pq, (3, 2): b_pq},
        {(0, False): c1, (0, True): d1, (-1, False): c2, (-1, True): d2, (2, False): c3, (2, True): d3}, after=[one],
    )
    rows = {
        (0, 0): a, (0, 2): b, (1, 0): a_p, (2, 0): a_q, (1, 2): b_p, (2, 2): b_q,
    }
    five = tile(rows, {(2, False): c3, (2, True): d3}, [one, two, three], after=[four])
    d4 = core_swap(c4)
    rows = {**rows, (3, 0): a_pq, (3, 2): b_pq}
    six = tile(rows, {(-3, False): c4}, [five, four])
    keep, give = tile(rows, {(-3, True): d4}, [six], spots=(0, 1, 2, 4, 3, 5, 6, 7))
    toward, back = call(
        cross_kernel, (shape(1, 1024, jnp.float32), shape(1, 128, jnp.float32)), [VMEM] * 4,
        [incoming, small, ids, target], [give], flops=2**28,
    )
    returned = pack_shift(back, -1)
    keep, give = fold(keep, over(give, "Q2"))
    keep, give = fold(keep, over(give, "P2"))
    keep, give = fold(keep, over(give, "Q"))
    giant_max = fold(keep, over(give, "P"))
    small_max = call(finish_kernel, shape(1, 1024, jnp.float32), [VMEM] * 4, [returned, send, local, toward])
    return giant_max.reshape(128), small_max.reshape(1024)


def solution(mesh):
    spread = P(AXES)
    wide = P(AXES, None)
    return jax.shard_map(
        body,
        mesh=mesh,
        in_specs=(wide, wide, spread, spread, spread),
        out_specs=(spread, spread),
        check_vma=False,
    )
```

```python
import functools
import jax
import jax.numpy as jnp
from jax import lax
from jax.experimental import pallas as pl
from jax.experimental.pallas import tpu as pltpu
from jax.sharding import PartitionSpec as P

AXES = ("row", "col", "pack")
LOW = -2.0
NT = (((1,), (1,)), ((), ()))
MIB = 1024 * 1024
SMEM = pl.BlockSpec(memory_space=pltpu.SMEM)
VMEM = pl.BlockSpec(memory_space=pltpu.VMEM)
LATER = pl.BlockSpec(memory_space=pl.ANY)


def place(x, y, z, c):
    return ((y * 2 + z // 4) * 8 + x * 2 + c) * 4 + z % 4


def z_step(z, odd):
    return (z + 1 + 6 * ((z + odd) % 2)) % 8


def partner(link, x, y, z, c):
    if link in ("E", "O"):
        return x, y, z_step(z, (link == "O") != (c == 1))
    flip = 1 if link[0] == "P" else 3
    along_x = (len(link) == 1) == (c == 0)
    return (x ^ flip, y, z) if along_x else (x, y ^ flip, z)


def route(move):
    cells = [(x, y, z, c) for x in range(4) for y in range(4) for z in range(8) for c in range(2)]
    return [(place(*cell), place(*move(*cell))) for cell in cells]


def over(block, link):
    return lax.ppermute(block, AXES, route(lambda x, y, z, c: (*partner(link, x, y, z, c), c)))


def core_swap(block):
    return lax.ppermute(block, AXES, route(lambda x, y, z, c: (x, y, z, 1 - c)))


def call(kernel, out_shape, specs, operands, after=(), flops=0, size=0):
    n = len(operands)

    def run(*refs):
        kernel(*refs[:n], *refs[n + len(after) :])

    many = isinstance(out_shape, (tuple, list))
    return pl.pallas_call(
        run,
        out_shape=out_shape,
        in_specs=list(specs) + [LATER] * len(after),
        out_specs=[VMEM] * len(out_shape) if many else VMEM,
        compiler_params=pltpu.CompilerParams(vmem_limit_bytes=8 * MIB),
        cost_estimate=pl.CostEstimate(flops=flops, bytes_accessed=size, transcendentals=0),
    )(*operands, *after)


def shape(rows, columns, dtype):
    return jax.ShapeDtypeStruct((rows, columns), dtype)


def dot_nt(left, right):
    total = None
    for k in range(0, 1024, 256):
        part = lax.dot_general(left[:, k : k + 256], right[:, k : k + 256], NT, preferred_element_type=jnp.float32)
        total = part if total is None else total + part
    return total


def unit_rows(values):
    wide = values.astype(jnp.float32)
    inverse = lax.rsqrt(jnp.sum(wide * wide, axis=-1, keepdims=True) + 1e-06)
    return (wide * inverse).astype(jnp.bfloat16)


def unit_kernel(values, out):
    for i in range(0, values.shape[0], 128):
        out[i : i + 128, :] = unit_rows(values[i : i + 128, :])


def join_kernel(first, second, out):
    rows = first.shape[0]
    out[:rows, :] = first[...]
    out[rows:, :] = second[...]


def join(first, second, after=()):
    rows = first.shape[0] + second.shape[0]
    return call(join_kernel, shape(rows, 1024, jnp.bfloat16), [VMEM] * 2, [first, second], after, size=rows * 4096)


def here():
    row_index, col_index, z_low = (lax.axis_index(a) for a in AXES)
    return col_index >> 1, row_index >> 1, ((row_index & 1) << 2) | z_low, col_index & 1


def first_row(x, y, z, c):
    return ((((((y << 1) | (z >> 2)) << 3) | (x << 1) | c) << 2) | (z & 3)) << 7


def plane_start(at, far, near):
    x, y, z, core = at
    flip = (0, 1, 3, 2)
    if far == near:
        along_x = along_y = flip[far]
    else:
        along_x = jnp.where(core == 0, flip[near], flip[far])
        along_y = jnp.where(core == 0, flip[far], flip[near])
    return first_row(x ^ along_x, y ^ along_y, z, core)


def line_start(at, steps, other):
    x, y, z, core = at
    core = (1 - core) if other else core
    way = 1 - 2 * ((z + core) & 1)
    return first_row(x, y, (z + way * steps + 8) & 7, core)


def tile_kernel(row_names, col_names, n_before, spots, *refs):
    at = here()
    n_r, n_c = len(row_names), len(col_names)
    r_refs, c_refs = refs[:n_r], refs[n_r : n_r + n_c]
    before, outs = refs[n_r + n_c : n_r + n_c + n_before], refs[n_r + n_c + n_before :]
    out_rows = outs[0].shape[0]
    lane = lax.broadcasted_iota(jnp.int32, (1, 256), 1)
    sub = lax.broadcasted_iota(jnp.int32, (128, 256), 0)
    starts = [[line_start(at, name + h if name >= 0 else name - h, other) for h in range(2)] for name, other in col_names]
    for j, (r_ref, (far, near)) in enumerate(zip(r_refs, row_names)):
        row_pos = jnp.where(lane < 128, plane_start(at, far, near) + lane, plane_start(at, far, near + 1) + lane - 128)
        best = jnp.full((8, 256), LOW, jnp.float32)
        for i in range(n_c):
            scores = dot_nt(c_refs[i], r_ref)
            for h in range(2):
                kept = jnp.where(sub < row_pos - starts[i][h], scores[128 * h : 128 * (h + 1)], LOW)
                best = jnp.maximum(best, jnp.max(kept.reshape(16, 8, 256), axis=0))
        best = jnp.max(best, axis=0, keepdims=True)
        for h in range(2):
            spot = 2 * j + h
            value = best[:, 128 * h : 128 * (h + 1)]
            seen = 0
            for b in before:
                if seen <= spot < seen + b.shape[0]:
                    value = jnp.maximum(value, b[spot - seen : spot - seen + 1, :])
                seen += b.shape[0]
            spot = 2 * spots[j] + h
            outs[spot // out_rows][spot % out_rows : spot % out_rows + 1, :] = value


def tile(rows, cols, before=(), after=(), spots=None):
    n = 2 * len(rows)
    out = shape(n, 128, jnp.float32) if spots is None else [shape(n // 2, 128, jnp.float32)] * 2
    operands = [*rows.values(), *cols.values(), *before]
    return call(
        functools.partial(tile_kernel, list(rows), list(cols), len(before), spots or range(len(rows))),
        out, [VMEM] * len(operands), operands, after,
        flops=2 * n * 128 * len(cols) * 256 * 1024, size=(n + 2 * len(cols)) * 256 * 1024,
    )


def fold_kernel(mine, theirs, *outs):
    best = jnp.maximum(mine[...], theirs[...])
    if len(outs) == 1:
        outs[0][...] = jnp.maximum(best, -1.0)
    else:
        half = best.shape[0] // 2
        outs[0][...] = best[:half]
        outs[1][...] = best[half:]


def fold(mine, theirs):
    half = mine.shape[0] // 2
    out = [shape(half, 128, jnp.float32)] * 2 if half else shape(1, 128, jnp.float32)
    return call(fold_kernel, out, [VMEM] * 2, [mine, theirs])


def column(row):
    return jnp.broadcast_to(row, (128, 128)).T


def gather_kernel(unit, send, out):
    lane = lax.broadcasted_iota(jnp.int32, (128, 128), 1)
    wanted = column(send[...])
    total = None
    for k in range(0, 1024, 256):
        hit = jnp.concatenate([wanted == lane + k, wanted == lane + k + 128], axis=1)
        part = jnp.dot(hit.astype(jnp.bfloat16), unit[k : k + 256, :], preferred_element_type=jnp.float32)
        total = part if total is None else total + part
    out[...] = total.astype(jnp.bfloat16)


def local_kernel(unit, ids, out):
    sub = lax.broadcasted_iota(jnp.int32, (256, 256), 0)
    lane = lax.broadcasted_iota(jnp.int32, (256, 256), 1)
    id_col = []
    for j in range(4):
        parts = [column(ids[:, 256 * j + 128 * h : 256 * j + 128 * (h + 1)]) for h in range(2)]
        part = jnp.concatenate(parts)
        id_col.append(jnp.concatenate([part, part], axis=1))
    for i in range(4):
        rows = slice(256 * i, 256 * (i + 1))
        best = jnp.full((8, 256), -1.0, jnp.float32)
        for j in range(i + 1):
            scores = dot_nt(unit[256 * j : 256 * (j + 1), :], unit[rows, :])
            allowed = id_col[j] == ids[:, rows]
            if i == j:
                allowed = allowed & (sub < lane)
            scores = jnp.where(allowed, scores, -1.0)
            best = jnp.maximum(best, jnp.max(scores.reshape(32, 8, 256), axis=0))
        out[:, rows] = jnp.max(best, axis=0, keepdims=True)


def cross_kernel(incoming, unit, ids, target, toward, back):
    lane = lax.broadcasted_iota(jnp.int32, (128, 128), 1)
    wanted = column(target[...])
    found = jnp.zeros((128, 128), jnp.int32)
    for k in range(0, 1024, 128):
        found = found + jnp.where(wanted == lane + k, ids[:, k : k + 128], 0)
    target_id = jnp.sum(found, axis=1, keepdims=True)
    back_best = jnp.full((128, 128), -1.0, jnp.float32)
    for i in range(0, 1024, 256):
        scores = dot_nt(incoming[...], unit[i : i + 256, :])
        scores = jnp.where(target_id == ids[:, i : i + 256], scores, -1.0)
        toward[:, i : i + 256] = jnp.max(scores, axis=0, keepdims=True)
        back_best = jnp.maximum(back_best, jnp.maximum(scores[:, :128], scores[:, 128:]))
    back[...] = jnp.max(back_best.T, axis=0, keepdims=True)


def finish_kernel(returned, send, local, toward, out):
    lane = lax.broadcasted_iota(jnp.int32, (128, 128), 1)
    wanted, value = column(send[...]), column(returned[...])
    for k in range(0, 1024, 128):
        hit = jnp.max(jnp.where(wanted == lane + k, value, -1.0), axis=0, keepdims=True)
        out[:, k : k + 128] = jnp.maximum(jnp.maximum(local[:, k : k + 128], toward[:, k : k + 128]), hit)


def pack_shift(block, distance):
    size = lax.axis_size("pack")
    return lax.ppermute(block, "pack", [((i - distance) % size, i) for i in range(size)])


def body(giant_emb, small_emb, small_ids, send_rows, target_rows):
    ids, send, target = small_ids.reshape(1, 1024), send_rows.reshape(1, 128), target_rows.reshape(1, 128)

    own = call(unit_kernel, shape(128, 1024, jnp.bfloat16), [VMEM], [giant_emb])
    e, p, q = over(own, "E"), over(own, "P"), over(own, "Q")
    small = call(unit_kernel, shape(1024, 1024, jnp.bfloat16), [VMEM], [small_emb], [own], size=4 * MIB)
    c1 = join(own, e, [small])
    c2, d1 = over(c1, "O"), core_swap(c1)
    a = join(own, p, [c1, q])
    pq = over(p, "Q")
    a_p, a_q = over(a, "P2"), over(a, "Q2")
    local = call(local_kernel, shape(1, 1024, jnp.float32), [VMEM] * 2, [small, ids], [a], flops=20 * 2**26)
    b = join(q, pq, [local])
    b_p, b_q = over(b, "P2"), over(b, "Q2")
    outgoing = call(gather_kernel, shape(128, 1024, jnp.bfloat16), [VMEM] * 2, [small, send], [b], flops=2**28)
    one = tile({(0, 0): a, (0, 2): b}, {(0, False): c1, (0, True): d1}, after=[outgoing])
    a_pq = over(a_p, "Q2")
    c3, d2 = over(c2, "E"), core_swap(c2)
    two = tile(
        {(1, 0): a_p, (2, 0): a_q}, {(0, False): c1, (0, True): d1, (-1, False): c2, (-1, True): d2}, after=[one],
    )
    b_pq = over(b_q, "P2")
    three = tile(
        {(1, 2): b_p, (2, 2): b_q}, {(0, False): c1, (0, True): d1, (-1, False): c2, (-1, True): d2}, after=[two],
    )
    one = tile({(0, 0): a, (0, 2): b}, {(-1, False): c2, (-1, True): d2}, [one], after=[three])
    c4, d3 = over(c3, "O"), core_swap(c3)
    incoming = pack_shift(outgoing, 1)
    four = tile(
        {(3, 0): a_pq, (3, 2): b_pq},
        {(0, False): c1, (0, True): d1, (-1, False): c2, (-1, True): d2, (2, False): c3, (2, True): d3}, after=[one],
    )
    rows = {
        (0, 0): a, (0, 2): b, (1, 0): a_p, (2, 0): a_q, (1, 2): b_p, (2, 2): b_q,
    }
    five = tile(rows, {(2, False): c3, (2, True): d3}, [one, two, three], after=[four])
    d4 = core_swap(c4)
    rows = {**rows, (3, 0): a_pq, (3, 2): b_pq}
    six = tile(rows, {(-3, False): c4}, [five, four])
    keep, give = tile(rows, {(-3, True): d4}, [six], spots=(0, 1, 2, 4, 3, 5, 6, 7))
    toward, back = call(
        cross_kernel, (shape(1, 1024, jnp.float32), shape(1, 128, jnp.float32)), [VMEM] * 4,
        [incoming, small, ids, target], [give], flops=2**28,
    )
    returned = pack_shift(back, -1)
    keep, give = fold(keep, over(give, "Q2"))
    keep, give = fold(keep, over(give, "P2"))
    keep, give = fold(keep, over(give, "Q"))
    giant_max = fold(keep, over(give, "P"))
    small_max = call(finish_kernel, shape(1, 1024, jnp.float32), [VMEM] * 4, [returned, send, local, toward])
    return giant_max.reshape(128), small_max.reshape(1024)


def solution(mesh):
    spread = P(AXES)
    wide = P(AXES, None)
    return jax.shard_map(
        body,
        mesh=mesh,
        in_specs=(wide, wide, spread, spread, spread),
        out_specs=(spread, spread),
        check_vma=False,
    )
```
